256 devices in a mesh: rows: 16 (over z_hi, y), cols: 16 (over x, z_lo, core).
Axes of the slice: x: 4, y: 4, z: 8 (z_hi: 4, z_lo: 2; z = z_hi * 2 + z_lo), core: 2. Of those that a mesh axis runs over, the one named last changes fastest.
Arguments:
- tiles: bfloat16 [2, 16, 16, 128, 128, 128], P(None, 'rows', 'cols'), may hold values from -0.078125 to 0.078125
- tile_scales: float32 [2, 16, 16, 128], P(None, 'rows', 'cols'), may hold values from 0.5 to 4
- tile_rows: int32 [2, 16, 16, 128], P(None, 'rows', 'cols'), may hold values from 0 to 7
- tile_cols: int32 [2, 16, 16, 128], P(None, 'rows', 'cols'), may hold values from 0 to 255
- tile_counts: int32 [2, 16, 16], P(None, 'rows', 'cols'), may hold values from 32 to 128, as said below
- labels: int32 [2, 16384], P(None, 'rows'), may hold values from 0 to 31
- learning_rate: float32 [2], replicated, may hold values from 4 to 16
- weights: float32 [32, 524288], P(None, ('cols', 'rows')), may hold values from -6 to 6
Outputs:
- trained: float32 [32, 524288], P(None, ('cols', 'rows'))
- losses: float32 [2, 16384], P(None, ('rows', 'cols'))
The draws below stay inside these ranges and needn't reach their ends.
Inputs may be any that keep to these rules, and one draw needn't show every extreme that they name: Only the first tile_counts[s, r, c] slots of a block are live; in every step some block has all 128 slots live.
All inputs are finite; a program needn't handle non-finite values.
Results may differ from the reference program's by a relative error of at most 0.0021.
Values may be sent and summed in bfloat16 or wider, within the bound.
No kernel may reach another device: no remote copies, remote signals or barrier semaphores. Data moves between devices by JAX's collectives and lax.ppermute only.
A program may use at most 64 MiB of HBM per device.

```python
import math
import jax
import jax.numpy as jnp
from jax import lax

CLASS_COUNT = 32
F = 524288
BLK = 128
STEPS = 2
STEP_SAMPLES = 1024
TILES = 128
SAMPLES = 16384
FB_DEV = 256
RB_DEV = 8
N_ROWS = 16
N_COLS = 16


def draw_tile_counts(key, part):
    shifts = jax.random.randint(key, (STEPS, N_ROWS * N_COLS), 0, 3)
    counts = TILES // jnp.left_shift(jnp.ones_like(shifts), shifts)
    fullest = jax.random.randint(jax.random.fold_in(key, 7), (STEPS, 1), 0, N_ROWS * N_COLS)
    places = jnp.arange(N_ROWS * N_COLS, dtype=jnp.int32)[None, :]
    counts = jnp.where(places == fullest, TILES, counts)
    return counts.reshape(STEPS, N_ROWS, N_COLS).astype(jnp.int32)


def set_ends(entries, rng, smallest, top_value):
    place = [jax.random.randint(jax.random.fold_in(rng, axis), (), 0, length) for axis, length in enumerate(entries.shape)]
    longest = entries.shape.index(max(entries.shape))
    next_to = place[:longest] + [(place[longest] + 1) % entries.shape[longest]] + place[longest + 1:]
    return entries.at[tuple(place)].set(smallest).at[tuple(next_to)].set(top_value)


def levels(rng, shape, pieces, low, top_value):
    gain = 1.0
    for position, shards_of in pieces:
        heights = jax.random.uniform(jax.random.fold_in(jax.random.fold_in(rng, 6), position), (shards_of,), jnp.float32, low / len(pieces), top_value / len(pieces))
        gain = gain * jnp.repeat(jnp.exp(heights), shape[position] // shards_of).reshape((-1,) + (1,) * (len(shape) - 1 - position))
    return gain


def scatter_about(own_key, extent, spread, bound, shards=(), kind=jnp.bfloat16):
    array = jax.random.normal(own_key, extent, jnp.float32) * spread
    if len(shards) > 0:
        array = levels(own_key, extent, shards, -0.22, 0.18) * array
    return jnp.clip(array, min=-bound, max=bound).astype(kind)


def setup_inputs(seed: int = 0) -> dict:
    key_of = jax.random.split(jax.random.key(seed), 9)
    tiles = scatter_about(key_of[0], (STEPS, N_ROWS, N_COLS, TILES, BLK, BLK), ((BLK * BLK * TILES * N_COLS // STEP_SAMPLES) ** -0.5), 0.078125, ((1, 16), (2, 16)))
    tile_scales = jnp.clip(jnp.exp(math.log(4.0) - 2.0794415 * jax.random.uniform(key_of[1], (STEPS, N_ROWS, N_COLS, TILES), jnp.float32) ** levels(key_of[1], (STEPS, N_ROWS, N_COLS, TILES), ((1, 16), (2, 16)), -0.2, 0.2)), 0.5, 4.0)
    tile_rows = set_ends(jax.random.randint(key_of[2], (STEPS, N_ROWS, N_COLS, TILES), 0, RB_DEV), jax.random.fold_in(key_of[2], 1), 0, RB_DEV - 1).astype(jnp.int32)
    tile_cols = set_ends(jax.random.randint(key_of[3], (STEPS, N_ROWS, N_COLS, TILES), 0, FB_DEV), jax.random.fold_in(key_of[3], 1), 0, FB_DEV - 1).astype(jnp.int32)
    tile_counts = draw_tile_counts(jax.random.fold_in(key_of[8], 71), 0)
    labels = set_ends(jax.random.randint(key_of[5], (STEPS, SAMPLES), 0, CLASS_COUNT), jax.random.fold_in(key_of[5], 1), 0, CLASS_COUNT - 1).astype(jnp.int32)
    learning_rate = jnp.clip(jnp.exp(jax.random.uniform(key_of[6], (STEPS,), jnp.float32, math.log(4.0), math.log(16.0))), 4.0, 16.0)
    weights = scatter_about(key_of[7], (CLASS_COUNT, F), 1.5, 6.0, ((1, 256),), jnp.float32)
    return dict(tiles=tiles, tile_scales=tile_scales, tile_rows=tile_rows, tile_cols=tile_cols, tile_counts=tile_counts, labels=labels, learning_rate=learning_rate, weights=weights)


def reference(tiles, tile_scales, tile_rows, tile_cols, tile_counts, labels, learning_rate, weights):
    col_blocks = F // (BLK * N_COLS)
    row_blocks = STEP_SAMPLES // BLK
    slot_ids = jnp.arange(TILES, dtype=jnp.int32)
    block_ids = jnp.arange(row_blocks, dtype=jnp.int32)
    class_ids = jnp.arange(CLASS_COUNT, dtype=jnp.int32)
    col_offsets = (jnp.arange(N_COLS, dtype=jnp.int32) * col_blocks)[:, None]
    current = weights
    losses = []
    for step_index in range(STEPS):
        wide_blocks = current.astype(jnp.bfloat16).reshape(CLASS_COUNT, F // BLK, BLK)

        def one_row(grad_sum, row_index):
            tile_entries = tiles[step_index][row_index].reshape(N_COLS * TILES, BLK, BLK).astype(jnp.float32)
            is_live = slot_ids[None, :] < tile_counts[step_index][row_index][:, None]
            factor = jnp.where(is_live, tile_scales[step_index][row_index], 0.0).reshape(-1)
            col_ids = (tile_cols[step_index][row_index] + col_offsets).reshape(-1).astype(jnp.int32)
            row_ids = tile_rows[step_index][row_index].reshape(-1).astype(jnp.int32)
            selected_entries = jnp.take(wide_blocks, col_ids, axis=1).astype(jnp.float32)
            weighted_products = jnp.einsum("zei,eui->ezu", selected_entries, tile_entries, precision=lax.Precision.HIGHEST)
            row_indicator = (row_ids[:, None] == block_ids[None, :]).astype(jnp.float32) * factor[:, None]
            class_scores = jnp.einsum("iu,idq->duq", row_indicator, weighted_products, precision=lax.Precision.HIGHEST).reshape(CLASS_COUNT, STEP_SAMPLES)
            step_labels = lax.dynamic_slice_in_dim(labels[step_index], (row_index * STEP_SAMPLES).astype(jnp.int32), STEP_SAMPLES)
            exp_logits = jnp.exp(class_scores)
            denominator = jnp.sum(exp_logits, axis=0)
            onehot = (class_ids[:, None] == step_labels[None, :]).astype(jnp.float32)
            sample_loss = jnp.log(denominator) - jnp.sum(onehot * class_scores, axis=0)
            residual = (exp_logits / denominator - onehot).astype(jnp.bfloat16)
            picked_rows = jnp.take(residual.reshape(CLASS_COUNT, row_blocks, BLK), row_ids, axis=1).astype(jnp.float32)
            grad_blocks = jnp.einsum("cts,tsf->ctf", picked_rows, tile_entries, precision=lax.Precision.HIGHEST) * factor[None, :, None]
            grad_sum = grad_sum.at[:, col_ids, :].add(grad_blocks)
            return grad_sum, sample_loss

        grad_sum, row_losses = lax.scan(one_row, jnp.zeros((CLASS_COUNT, F // BLK, BLK), jnp.float32), jnp.arange(N_ROWS, dtype=jnp.int32))
        current = current - learning_rate[step_index] * grad_sum.reshape(CLASS_COUNT, F)
        losses.append(row_losses.reshape(-1))
    return current, jnp.stack(losses)
```

```python
import functools

import jax
import jax.numpy as jnp
from jax import lax
from jax.experimental import pallas as pl
from jax.experimental.pallas import tpu as pltpu
from jax.sharding import PartitionSpec as P

CLASSES = 32
TILE = 128
SLOTS = 128
GROUP = 16
ROW_BLOCKS = 8
OWN_BLOCKS = 16
PIECE = OWN_BLOCKS * CLASSES
LIMIT = 28 * 1024 * 1024

VMEM = pltpu.VMEM
SMEM = pltpu.SMEM


def y_shift(value, k):
    perm = [(z * 4 + y, z * 4 + (y + k) % 4) for z in range(4) for y in range(4)]
    return lax.ppermute(value, "rows", perm)


def z_shift(value, k):
    perm = [(z * 4 + y, (z + k) % 4 * 4 + y) for z in range(4) for y in range(4)]
    return lax.ppermute(value, "rows", perm)


def x_shift(value, k):
    perm = [(x * 4 + j, (x + k) % 4 * 4 + j) for x in range(4) for j in range(4)]
    return lax.ppermute(value, "cols", perm)


def flip(value, bit):
    return lax.ppermute(value, "cols", [(i, i ^ bit) for i in range(16)])


def vmem():
    return pl.BlockSpec(memory_space=VMEM)


def smem():
    return pl.BlockSpec(memory_space=SMEM)


def params():
    return pltpu.CompilerParams(vmem_limit_bytes=LIMIT)


def block_kernel(w_ref, out_ref):
    for b in range(OWN_BLOCKS):
        out_ref[pl.ds(b * CLASSES, CLASSES), :] = w_ref[:, pl.ds(b * TILE, TILE)].astype(
            jnp.bfloat16
        )


def to_blocks(weights):
    return pl.pallas_call(
        block_kernel,
        out_shape=jax.ShapeDtypeStruct((PIECE, TILE), jnp.bfloat16),
        in_specs=[vmem()],
        out_specs=vmem(),
        compiler_params=params(),
        name="to_blocks",
    )(weights)


def tile_spec(step):
    return pl.BlockSpec(
        (None, None, None, GROUP, TILE, TILE), lambda g: (step, 0, 0, g, 0, 0)
    )


def logits_kernel(step, count_ref, place_ref, row_ref, scale_ref, tiles_ref, *rest):
    pieces, out_ref, wide = rest[:4], rest[4], rest[5]
    group = pl.program_id(0)

    @pl.when(group == 0)
    def _():
        for j, piece in enumerate(pieces):
            wide[pl.ds(j * 4 * OWN_BLOCKS, 4 * OWN_BLOCKS)] = piece[...].reshape(
                4 * OWN_BLOCKS, CLASSES, TILE
            )
        out_ref[...] = jnp.zeros_like(out_ref)

    count = count_ref[step]

    @pl.when(group * GROUP < count)
    def _():
        products = []
        for u in range(GROUP):
            slot = group * GROUP + u
            products.append(
                lax.dot_general(
                    wide[place_ref[step * SLOTS + slot]],
                    tiles_ref[u],
                    (((1,), (1,)), ((), ())),
                    preferred_element_type=jnp.float32,
                )
            )
        for u in range(GROUP):
            slot = group * GROUP + u
            factor = jnp.where(slot < count, scale_ref[step * SLOTS + slot], 0.0)
            out_ref[row_ref[step * SLOTS + slot]] += factor * products[u]


def partial_logits(step, meta, tiles, pieces):
    return pl.pallas_call(
        functools.partial(logits_kernel, step),
        grid=(SLOTS // GROUP,),
        out_shape=jax.ShapeDtypeStruct((ROW_BLOCKS, CLASSES, TILE), jnp.float32),
        in_specs=[smem()] * 4 + [tile_spec(step)] + [vmem()] * 4,
        out_specs=vmem(),
        scratch_shapes=[VMEM((256, CLASSES, TILE), jnp.bfloat16)],
        compiler_params=params(),
        name="partial_logits",
    )(meta["counts"], meta["from"], meta["rows"], meta["scales"], tiles, *pieces)


def gradient_kernel(step, count_ref, place_ref, row_ref, scale_ref, tiles_ref, label_ref, *rest):
    parts, loss_ref, own_ref, far_refs, total, residual = (
        rest[:4], rest[4], rest[5], rest[6:9], rest[9], rest[10]
    )
    group = pl.program_id(0)

    @pl.when(group == 0)
    def _():
        total[...] = jnp.zeros_like(total)
        for block in range(ROW_BLOCKS):
            scores = (parts[0][block] + parts[1][block]) + (parts[2][block] + parts[3][block])
            label = label_ref[pl.ds(step * ROW_BLOCKS + block, 1), :]
            hit = lax.broadcasted_iota(jnp.int32, (CLASSES, TILE), 0) == label
            exps = jnp.exp(scores)
            denominator = jnp.sum(exps, axis=0, keepdims=True)
            picked = jnp.sum(jnp.where(hit, scores, 0.0), axis=0, keepdims=True)
            loss_ref[pl.ds(block, 1), :] = jnp.log(denominator) - picked
            residual[block] = (exps / denominator - hit.astype(jnp.float32)).astype(jnp.bfloat16)

    count = count_ref[step]

    @pl.when(group * GROUP < count)
    def _():
        products = []
        for u in range(GROUP):
            slot = group * GROUP + u
            products.append(
                lax.dot_general(
                    residual[row_ref[step * SLOTS + slot]],
                    tiles_ref[u],
                    (((1,), (0,)), ((), ())),
                    preferred_element_type=jnp.float32,
                )
            )
        for u in range(GROUP):
            slot = group * GROUP + u
            factor = jnp.where(slot < count, scale_ref[step * SLOTS + slot], 0.0)
            total[place_ref[step * SLOTS + slot]] += factor * products[u]

    @pl.when(group == SLOTS // GROUP - 1)
    def _():
        span = 4 * OWN_BLOCKS
        own_ref[...] = total[pl.ds(0, span)].reshape(4 * PIECE, TILE)
        for j in range(3):
            far_refs[j][...] = (
                total[pl.ds((j + 1) * span, span)].reshape(4 * PIECE, TILE).astype(jnp.bfloat16)
            )


def gradient(step, meta, tiles, labels, parts):
    far = jax.ShapeDtypeStruct((4 * PIECE, TILE), jnp.bfloat16)
    return pl.pallas_call(
        functools.partial(gradient_kernel, step),
        grid=(SLOTS // GROUP,),
        out_shape=[
            jax.ShapeDtypeStruct((ROW_BLOCKS, TILE), jnp.float32),
            jax.ShapeDtypeStruct((4 * PIECE, TILE), jnp.float32),
            far,
            far,
            far,
        ],
        in_specs=[smem()] * 4 + [tile_spec(step)] + [vmem()] * 5,
        out_specs=[vmem()] * 5,
        scratch_shapes=[
            VMEM((256, CLASSES, TILE), jnp.float32),
            VMEM((ROW_BLOCKS, CLASSES, TILE), jnp.bfloat16),
        ],
        compiler_params=params(),
        name="gradient",
    )(meta["counts"], meta["to"], meta["rows"], meta["scales"], tiles, labels, *parts)


def fold_kernel(own_ref, a_ref, b_ref, c_ref, near_ref, *far_refs):
    for i in range(4):
        rows = pl.ds(i * PIECE, PIECE)
        value = own_ref[rows, :] + (
            a_ref[rows, :].astype(jnp.float32)
            + b_ref[rows, :].astype(jnp.float32)
            + c_ref[rows, :].astype(jnp.float32)
        )
        if i == 0:
            near_ref[...] = value
        else:
            far_refs[i - 1][...] = value.astype(jnp.bfloat16)


def fold(own, received):
    far = jax.ShapeDtypeStruct((PIECE, TILE), jnp.bfloat16)
    return pl.pallas_call(
        fold_kernel,
        out_shape=[jax.ShapeDtypeStruct((PIECE, TILE), jnp.float32), far, far, far],
        in_specs=[vmem()] * 4,
        out_specs=[vmem()] * 4,
        compiler_params=params(),
        name="fold",
    )(own, *received)


def update_kernel(step, rate_ref, w_ref, near_ref, a_ref, b_ref, c_ref, out_ref, *wide_ref):
    rate = rate_ref[step]
    for b in range(OWN_BLOCKS):
        rows = pl.ds(b * CLASSES, CLASSES)
        value = near_ref[rows, :] + (
            a_ref[rows, :].astype(jnp.float32)
            + b_ref[rows, :].astype(jnp.float32)
            + c_ref[rows, :].astype(jnp.float32)
        )
        new = w_ref[:, pl.ds(b * TILE, TILE)] - rate * value
        out_ref[:, pl.ds(b * TILE, TILE)] = new
        for ref in wide_ref:
            ref[rows, :] = new.astype(jnp.bfloat16)


def update(step, rate, weights, near, received, last):
    out_shape = [jax.ShapeDtypeStruct(weights.shape, jnp.float32)]
    if not last:
        out_shape.append(jax.ShapeDtypeStruct((PIECE, TILE), jnp.bfloat16))
    return pl.pallas_call(
        functools.partial(update_kernel, step),
        out_shape=out_shape,
        in_specs=[smem()] + [vmem()] * 5,
        out_specs=[vmem()] * len(out_shape),
        compiler_params=params(),
        name="update",
    )(rate, weights, near, *received)


def per_device(
    tiles, tile_scales, tile_rows, tile_cols, tile_counts, labels, learning_rate, weights
):
    steps = tiles.shape[0]
    place = lax.axis_index("rows")
    z, y = place // 4, place % 4
    owner, within = tile_cols.reshape(-1) // OWN_BLOCKS, tile_cols.reshape(-1) % OWN_BLOCKS
    dz, dy = z - owner // 4, y - owner % 4
    meta = dict(
        counts=tile_counts.reshape(-1),
        rows=tile_rows.reshape(-1),
        scales=tile_scales.reshape(-1),
    )
    meta["from"] = ((dy & 3) * 4 + (dz & 3)) * OWN_BLOCKS + within
    meta["to"] = ((-dy & 3) * 4 + (-dz & 3)) * OWN_BLOCKS + within
    label_rows = labels.reshape(steps * ROW_BLOCKS, TILE)
    samples = labels.shape[1]
    owned = samples // lax.axis_size("cols")
    start = lax.axis_index("cols") * owned

    losses = []
    wide = to_blocks(weights)
    for step in range(steps):
        near = jnp.concatenate([wide] + [z_shift(wide, k) for k in (1, 2, 3)])
        pieces = [near] + [y_shift(near, k) for k in (1, 2, 3)]
        part = partial_logits(step, meta, tiles, pieces)
        part = part + flip(part, 1)
        part = part + flip(part, 2)
        parts = [part] + [x_shift(part, k) for k in (1, 2, 3)]
        loss, own, *far = gradient(step, meta, tiles, label_rows, parts)
        losses.append(lax.dynamic_slice_in_dim(loss.reshape(-1), start, owned))
        received = [y_shift(far[k - 1], k) for k in (1, 2, 3)]
        near, *far = fold(own, received)
        received = [z_shift(far[k - 1], k) for k in (1, 2, 3)]
        weights, *wide = update(
            step, learning_rate, weights, near, received, step == steps - 1
        )
        wide = wide[0] if wide else None
    return weights, jnp.stack(losses)


def solution(mesh):
    return jax.shard_map(
        per_device,
        mesh=mesh,
        in_specs=(
            P(None, "rows", "cols", None, None, None),
            P(None, "rows", "cols", None),
            P(None, "rows", "cols", None),
            P(None, "rows", "cols", None),
            P(None, "rows", "cols"),
            P(None, "rows"),
            P(),
            P(None, ("cols", "rows")),
        ),
        out_specs=(P(None, ("cols", "rows")), P(None, ("rows", "cols"))),
        check_vma=False,
    )
```

```python
import functools

import jax
import jax.numpy as jnp
from jax import lax
from jax.experimental import pallas as pl
from jax.experimental.pallas import tpu as pltpu
from jax.sharding import PartitionSpec as P

CLASSES = 32
TILE = 128
SLOTS = 128
GROUP = 16
GROUPS = SLOTS // GROUP
ROW_BLOCKS = 8
OWN_ROW_BLOCKS = 4
OWN_BLOCKS = 16
PIECE = OWN_BLOCKS * CLASSES
LINE = 4 * PIECE
HALF = LINE // 2
LIMIT = 28 * 1024 * 1024

VMEM = pltpu.VMEM
F32 = jnp.float32
BF16 = jnp.bfloat16


def y_shift(value, k):
    perm = [(z * 4 + y, z * 4 + (y + k) % 4) for z in range(4) for y in range(4)]
    return lax.ppermute(value, "rows", perm)


def z_shift(value, k):
    perm = [(z * 4 + y, (z + k) % 4 * 4 + y) for z in range(4) for y in range(4)]
    return lax.ppermute(value, "rows", perm)


def x_shift(value, k):
    perm = [(x * 4 + j, (x + k) % 4 * 4 + j) for x in range(4) for j in range(4)]
    return lax.ppermute(value, "cols", perm)


def flip(value, bit):
    return lax.ppermute(value, "cols", [(i, i ^ bit) for i in range(16)])


def vmem():
    return pl.BlockSpec(memory_space=VMEM)


def smem():
    return pl.BlockSpec(memory_space=pltpu.SMEM)


def hbm():
    return pl.BlockSpec(memory_space=pltpu.HBM)


def call(kernel, name, outs, ins, scratch=()):
    return pl.pallas_call(
        kernel,
        out_shape=[jax.ShapeDtypeStruct(shape, dtype) for shape, dtype in outs],
        in_specs=ins,
        out_specs=[vmem()] * len(outs),
        scratch_shapes=list(scratch),
        compiler_params=pltpu.CompilerParams(vmem_limit_bytes=LIMIT),
        name=name,
    )


def block_kernel(w_ref, out_ref):
    for b in range(OWN_BLOCKS):
        out_ref[pl.ds(b * CLASSES, CLASSES), :] = w_ref[:, pl.ds(b * TILE, TILE)].astype(BF16)


def to_blocks(weights):
    return call(block_kernel, "to_blocks", [((PIECE, TILE), BF16)], [vmem()])(weights)[0]


def tile_copy(step, tiles_ref, held, sems, group):
    part = pl.ds(group * GROUP, GROUP)
    return pltpu.make_async_copy(tiles_ref.at[step, 0, 0, part], held.at[part], sems.at[group])


TILE_SCRATCH = (VMEM((SLOTS, TILE, TILE), BF16), pltpu.SemaphoreType.DMA((GROUPS,)))


def logits_kernel(step, code_ref, factor_ref, tiles_ref, *rest):
    near, back, ahead, far_low, far_high, mine_ref, other_ref, total, wide, held, sems = rest
    for group in range(GROUPS):
        tile_copy(step, tiles_ref, held, sems, group).start()
    span = 4 * OWN_BLOCKS
    for j, piece in ((0, near), (1, back), (3, ahead)):
        wide[pl.ds(j * span, span)] = piece[...].reshape(span, CLASSES, TILE)
    wide[pl.ds(2 * span, span // 2)] = far_low[...].reshape(span // 2, CLASSES, TILE)
    wide[pl.ds(2 * span + span // 2, span // 2)] = far_high[...].reshape(
        span // 2, CLASSES, TILE
    )
    total[...] = jnp.zeros_like(total)

    def body(group, carry):
        tile_copy(step, tiles_ref, held, sems, group).wait()
        start = group * GROUP
        codes = [code_ref[step * SLOTS + start + u] for u in range(GROUP)]
        products = [
            lax.dot_general(
                wide[codes[u] & 255],
                held[start + u],
                (((1,), (1,)), ((), ())),
                preferred_element_type=F32,
            )
            for u in range(GROUP)
        ]
        for u in range(GROUP):
            total[codes[u] >> 16] += factor_ref[step * SLOTS + start + u] * products[u]
        return carry

    lax.fori_loop(0, GROUPS, body, 0)
    mine_ref[...] = total[pl.ds(0, OWN_ROW_BLOCKS)]
    other_ref[...] = total[pl.ds(OWN_ROW_BLOCKS, OWN_ROW_BLOCKS)]


def partial_logits(step, code, factor, tiles, pieces):
    half = ((OWN_ROW_BLOCKS, CLASSES, TILE), F32)
    return call(
        functools.partial(logits_kernel, step),
        "partial_logits",
        [half, half],
        [smem(), smem(), hbm()] + [vmem()] * 5,
        [VMEM((ROW_BLOCKS, CLASSES, TILE), F32), VMEM((256, CLASSES, TILE), BF16), *TILE_SCRATCH],
    )(code, factor, tiles, *pieces)


def classify_kernel(step, a_ref, b_ref, c_ref, d_ref, label_ref, residual_ref, loss_ref):
    for block in range(OWN_ROW_BLOCKS):
        scores = (a_ref[block] + b_ref[block]) + (c_ref[block] + d_ref[block])
        label = label_ref[pl.ds(step * OWN_ROW_BLOCKS + block, 1), :]
        hit = lax.broadcasted_iota(jnp.int32, (CLASSES, TILE), 0) == label
        exps = jnp.exp(scores)
        denominator = jnp.sum(exps, axis=0, keepdims=True)
        picked = jnp.sum(jnp.where(hit, scores, 0.0), axis=0, keepdims=True)
        loss_ref[pl.ds(block, 1), :] = jnp.log(denominator) - picked
        residual_ref[block] = (exps / denominator - hit.astype(F32)).astype(BF16)


def classify(step, parts, labels):
    return call(
        functools.partial(classify_kernel, step),
        "classify",
        [((OWN_ROW_BLOCKS, CLASSES, TILE), BF16), ((OWN_ROW_BLOCKS, TILE), F32)],
        [vmem()] * 5,
    )(*parts, labels)


def gradient_kernel(step, code_ref, factor_ref, tiles_ref, mine_ref, other_ref, *rest):
    outs, (total, residual, held, sems) = rest[:7], rest[7:]
    near, up_keep, up_send, far_low, far_high, down_send, down_keep = outs
    for group in range(GROUPS):
        tile_copy(step, tiles_ref, held, sems, group).start()
    residual[pl.ds(0, OWN_ROW_BLOCKS)] = mine_ref[...]
    residual[pl.ds(OWN_ROW_BLOCKS, OWN_ROW_BLOCKS)] = other_ref[...]
    total[...] = jnp.zeros_like(total)

    def body(group, carry):
        tile_copy(step, tiles_ref, held, sems, group).wait()
        start = group * GROUP
        codes = [code_ref[step * SLOTS + start + u] for u in range(GROUP)]
        products = [
            lax.dot_general(
                residual[codes[u] >> 16],
                held[start + u],
                (((1,), (0,)), ((), ())),
                preferred_element_type=F32,
            )
            for u in range(GROUP)
        ]
        for u in range(GROUP):
            total[(codes[u] >> 8) & 255] += factor_ref[step * SLOTS + start + u] * products[u]
        return carry

    lax.fori_loop(0, GROUPS, body, 0)
    span = 2 * OWN_BLOCKS
    near[...] = total[pl.ds(0, 2 * span)].reshape(LINE, TILE)
    for k, ref in enumerate((up_keep, up_send, far_low, far_high, down_send, down_keep)):
        ref[...] = total[pl.ds((k + 2) * span, span)].reshape(HALF, TILE).astype(ref.dtype)


def gradient(step, code, factor, tiles, mine, other):
    send, keep = ((HALF, TILE), BF16), ((HALF, TILE), F32)
    return call(
        functools.partial(gradient_kernel, step),
        "gradient",
        [((LINE, TILE), F32), keep, send, send, send, send, keep],
        [smem(), smem(), hbm()] + [vmem()] * 2,
        [
            VMEM((256, CLASSES, TILE), F32),
            VMEM((ROW_BLOCKS, CLASSES, TILE), BF16),
            *TILE_SCRATCH,
        ],
    )(code, factor, tiles, mine, other)


def relay_kernel(keep_ref, came_ref, out_ref):
    out_ref[...] = (keep_ref[...] + came_ref[...].astype(F32)).astype(BF16)


def relay(keep, came):
    return call(relay_kernel, "relay", [((HALF, TILE), BF16)], [vmem()] * 2)(keep, came)[0]


def fold_kernel(own_ref, low_a, low_b, high_a, high_b, near_ref, *far_refs):
    for i in range(4):
        a_ref, b_ref = ((low_a, low_b), (high_a, high_b))[i // 2]
        rows = pl.ds(i % 2 * PIECE, PIECE)
        value = own_ref[pl.ds(i * PIECE, PIECE), :] + (
            a_ref[rows, :].astype(F32) + b_ref[rows, :].astype(F32)
        )
        if i == 0:
            near_ref[...] = value
        else:
            far_refs[i - 1][...] = value.astype(BF16)


def fold(own, *received):
    far = ((PIECE, TILE), BF16)
    return call(
        fold_kernel, "fold", [((PIECE, TILE), F32), far, far, far], [vmem()] * 5
    )(own, *received)


def update_kernel(step, rate_ref, w_ref, near_ref, a_ref, b_ref, c_ref, out_ref, *wide_ref):
    rate = rate_ref[step]
    for b in range(OWN_BLOCKS):
        rows = pl.ds(b * CLASSES, CLASSES)
        value = near_ref[rows, :] + (
            a_ref[rows, :].astype(F32) + b_ref[rows, :].astype(F32) + c_ref[rows, :].astype(F32)
        )
        new = w_ref[:, pl.ds(b * TILE, TILE)] - rate * value
        out_ref[:, pl.ds(b * TILE, TILE)] = new
        for ref in wide_ref:
            ref[rows, :] = new.astype(BF16)


def update(step, rate, weights, near, received, last):
    outs = [(weights.shape, F32)]
    if not last:
        outs.append(((PIECE, TILE), BF16))
    return call(
        functools.partial(update_kernel, step), "update", outs, [smem()] + [vmem()] * 5
    )(rate, weights, near, *received)


def per_device(
    tiles, tile_scales, tile_rows, tile_cols, tile_counts, labels, learning_rate, weights
):
    steps = tiles.shape[0]
    place = lax.axis_index("rows")
    core = lax.axis_index("cols") % 2
    z, y = place // 4, place % 4
    columns = tile_cols.reshape(steps, SLOTS)
    owner, within = columns // OWN_BLOCKS, columns % OWN_BLOCKS
    dz, dy = z - owner // 4, y - owner % 4
    source = ((dy & 3) * 4 + (dz & 3)) * OWN_BLOCKS + within
    target = ((-dy & 3) * 4 + (-dz & 3)) * OWN_BLOCKS + within
    block = (tile_rows.reshape(steps, SLOTS) + OWN_ROW_BLOCKS * core) & (ROW_BLOCKS - 1)
    code = (source + (target << 8) + (block << 16)).reshape(-1)
    live = jnp.arange(SLOTS, dtype=jnp.int32)[None, :] < tile_counts.reshape(steps, 1)
    factor = jnp.where(live, tile_scales.reshape(steps, SLOTS), 0.0).reshape(-1)
    own_labels = lax.dynamic_slice_in_dim(
        labels.reshape(steps, ROW_BLOCKS, TILE), core * OWN_ROW_BLOCKS, OWN_ROW_BLOCKS, axis=1
    ).reshape(steps * OWN_ROW_BLOCKS, TILE)
    owned = labels.shape[1] // lax.axis_size("cols")
    start = lax.axis_index("cols") * owned

    losses = []
    wide = to_blocks(weights)
    for step in range(steps):
        near = jnp.concatenate([wide] + [z_shift(wide, k) for k in (1, 2, 3)])
        back, ahead = y_shift(near, 1), y_shift(near, -1)
        pieces = (near, back, ahead, y_shift(back[:HALF], 1), y_shift(ahead[HALF:], -1))
        mine, other = partial_logits(step, code, factor, tiles, pieces)
        mine = mine + flip(other, 1)
        mine = mine + flip(mine, 2)
        parts = [mine] + [x_shift(mine, k) for k in (1, 2, 3)]
        mine, loss = classify(step, parts, own_labels)
        losses.append(loss)
        grads = gradient(step, code, factor, tiles, mine, flip(mine, 1))
        own, up_keep, up_send, far_low, far_high, down_send, down_keep = grads
        via_low, via_high = y_shift(far_low, 1), y_shift(far_high, -1)
        high_a, low_a = y_shift(up_send, 1), y_shift(down_send, -1)
        low_b = y_shift(relay(up_keep, via_low), 1)
        high_b = y_shift(relay(down_keep, via_high), -1)
        near, *far = fold(own, low_a, low_b, high_a, high_b)
        received = [z_shift(far[k - 1], k) for k in (1, 2, 3)]
        weights, *wide = update(
            step, learning_rate, weights, near, received, step == steps - 1
        )
        wide = wide[0] if wide else None

    loss = jnp.stack(losses)
    there = flip(loss, 1)
    first = core == 0
    loss = jnp.concatenate([jnp.where(first, loss, there), jnp.where(first, there, loss)], axis=1)
    loss = lax.dynamic_slice_in_dim(loss.reshape(steps, -1), start, owned, axis=1)
    return weights, loss


def solution(mesh):
    return jax.shard_map(
        per_device,
        mesh=mesh,
        in_specs=(
            P(None, "rows", "cols", None, None, None),
            P(None, "rows", "cols", None),
            P(None, "rows", "cols", None),
            P(None, "rows", "cols", None),
            P(None, "rows", "cols"),
            P(None, "rows"),
            P(),
            P(None, ("cols", "rows")),
        ),
        out_specs=(P(None, ("cols", "rows")), P(None, ("rows", "cols"))),
        check_vma=False,
    )
```

```python
import functools

import jax
import jax.numpy as jnp
from jax import lax
from jax.experimental import pallas as pl
from jax.experimental.pallas import tpu as pltpu
from jax.sharding import PartitionSpec as P

CLASSES = 32
TILE = 128
SLOTS = 128
GROUP = 16
GROUPS = SLOTS // GROUP
FAR = 192
ROW_BLOCKS = 8
OWN_ROW_BLOCKS = 4
OWN_BLOCKS = 16
PIECE = OWN_BLOCKS * CLASSES
LINE = 4 * PIECE
HALF = LINE // 2
LIMIT = 20 * 1024 * 1024
SLOT_LIMIT = 46 * 1024 * 1024

STEPS = 2
VMEM = pltpu.VMEM
COST = pl.CostEstimate(flops=1 << 30, bytes_accessed=1 << 23, transcendentals=0)
F32 = jnp.float32
BF16 = jnp.bfloat16


def y_shift(value, k):
    perm = [(z * 4 + y, z * 4 + (y + k) % 4) for z in range(4) for y in range(4)]
    return lax.ppermute(value, "rows", perm)


def z_shift(value, k):
    perm = [(z * 4 + y, (z + k) % 4 * 4 + y) for z in range(4) for y in range(4)]
    return lax.ppermute(value, "rows", perm)


def x_shift(value, k):
    perm = [(x * 4 + j, (x + k) % 4 * 4 + j) for x in range(4) for j in range(4)]
    return lax.ppermute(value, "cols", perm)


def flip(value, bit):
    return lax.ppermute(value, "cols", [(i, i ^ bit) for i in range(16)])


def vmem():
    return pl.BlockSpec(memory_space=VMEM)


def smem():
    return pl.BlockSpec(memory_space=pltpu.SMEM)


def hbm():
    return pl.BlockSpec(memory_space=pltpu.HBM)


def call(kernel, name, outs, ins, scratch=(), limit=LIMIT, cost=None):
    return pl.pallas_call(
        kernel,
        out_shape=[jax.ShapeDtypeStruct(shape, dtype) for shape, dtype in outs],
        in_specs=ins,
        out_specs=[vmem()] * len(outs),
        scratch_shapes=list(scratch),
        compiler_params=pltpu.CompilerParams(vmem_limit_bytes=limit),
        cost_estimate=cost,
        name=name,
    )


def block_kernel(w_ref, out_ref):
    for b in range(OWN_BLOCKS):
        out_ref[pl.ds(b * CLASSES, CLASSES), :] = w_ref[:, pl.ds(b * TILE, TILE)].astype(BF16)


def to_blocks(weights):
    return call(block_kernel, "to_blocks", [((PIECE, TILE), BF16)], [vmem()])(weights)[0]


def over_slots(order, step, first, code_ref, factor_ref, bound_ref, product, add, ready=None):
    row = order * STEPS + step
    low = 0 if first else bound_ref[2 * row]
    high = bound_ref[2 * row] if first else bound_ref[2 * row + 1]

    def body(group, carry):
        if ready is not None:
            ready(group)
        codes, factors = [], []
        for u in range(GROUP):
            place = low + group * GROUP + u
            entry = row * SLOTS + jnp.minimum(place, SLOTS - 1)
            codes.append(code_ref[entry])
            factors.append(jnp.where(place < high, factor_ref[entry], 0.0))
        products = [product(code & 255, (code >> 8) & 7, code >> 11) for code in codes]
        for code, factor, value in zip(codes, factors, products):
            add(code & 255, (code >> 8) & 7, factor * value)
        return carry

    groups = (high - low + GROUP - 1) // GROUP
    lax.fori_loop(0, groups, body, 0)
    return groups


def tile_copy(step, tiles_ref, held, sems, group):
    part = pl.ds(group * GROUP, GROUP)
    return pltpu.make_async_copy(tiles_ref.at[step, 0, 0, part], held.at[part], sems.at[group])


def logits_kernel(step, code_ref, factor_ref, bound_ref, tiles_ref, *rest):
    pieces, (mine_ref, other_ref, held, total, wide, sems) = rest[:16], rest[16:]
    for group in range(GROUPS):
        tile_copy(step, tiles_ref, held, sems, group).start()
    for j, piece in enumerate(pieces):
        wide[pl.ds(j * OWN_BLOCKS, OWN_BLOCKS)] = piece[...].reshape(OWN_BLOCKS, CLASSES, TILE)
    total[...] = jnp.zeros_like(total)

    def product(place, block, slot):
        return lax.dot_general(
            wide[place], held[slot], (((1,), (1,)), ((), ())), preferred_element_type=F32
        )

    def add(place, block, value):
        total[block] += value

    def wait(group, carry=0):
        tile_copy(step, tiles_ref, held, sems, group).wait()
        return carry

    done = over_slots(0, step, True, code_ref, factor_ref, bound_ref, product, add, wait)
    lax.fori_loop(done, GROUPS, wait, 0)
    mine_ref[...] = total[pl.ds(0, OWN_ROW_BLOCKS)]
    other_ref[...] = total[pl.ds(OWN_ROW_BLOCKS, OWN_ROW_BLOCKS)]


def partial_logits(step, meta, tiles, pieces):
    half = ((OWN_ROW_BLOCKS, CLASSES, TILE), F32)
    return call(
        functools.partial(logits_kernel, step),
        "partial_logits",
        [half, half, ((SLOTS, TILE, TILE), BF16)],
        [smem()] * 3 + [hbm()] + [vmem()] * 16,
        [
            VMEM((ROW_BLOCKS, CLASSES, TILE), F32),
            VMEM((256, CLASSES, TILE), BF16),
            pltpu.SemaphoreType.DMA((GROUPS,)),
        ],
        SLOT_LIMIT,
    )(*meta, tiles, *pieces)


def classify_kernel(step, core_ref, a_ref, b_ref, c_ref, d_ref, label_ref, *outs):
    residual_ref, loss_ref = outs
    for block in range(OWN_ROW_BLOCKS):
        scores = (a_ref[block] + b_ref[block]) + (c_ref[block] + d_ref[block])
        first = (core_ref[0] * OWN_ROW_BLOCKS + block) * TILE
        label = label_ref[pl.ds(step, 1), pl.ds(pl.multiple_of(first, TILE), TILE)]
        hit = lax.broadcasted_iota(jnp.int32, (CLASSES, TILE), 0) == label
        exps = jnp.exp(scores)
        denominator = jnp.sum(exps, axis=0, keepdims=True)
        picked = jnp.sum(jnp.where(hit, scores, 0.0), axis=0, keepdims=True)
        loss_ref[pl.ds(block, 1), :] = jnp.log(denominator) - picked
        residual_ref[block] = (exps / denominator - hit.astype(F32)).astype(BF16)


def classify(step, core, parts, labels):
    return call(
        functools.partial(classify_kernel, step),
        "classify",
        [((OWN_ROW_BLOCKS, CLASSES, TILE), BF16), ((OWN_ROW_BLOCKS, TILE), F32)],
        [smem()] + [vmem()] * 5,
    )(core, *parts, labels)


def gradient_kernel(first, step, code_ref, factor_ref, bound_ref, held, mine_ref, other_ref, *rest):
    outs, (total, residual) = rest[:-2], rest[-2:]
    residual[pl.ds(0, OWN_ROW_BLOCKS)] = mine_ref[...]
    residual[pl.ds(OWN_ROW_BLOCKS, OWN_ROW_BLOCKS)] = other_ref[...]
    total[...] = jnp.zeros_like(total)

    def product(place, block, slot):
        return lax.dot_general(
            residual[block], held[slot], (((1,), (0,)), ((), ())), preferred_element_type=F32
        )

    def add(place, block, value):
        place = jnp.maximum(place - FAR, 0) if first else jnp.minimum(place, FAR - 1)
        total[place] += value

    over_slots(1, step, first, code_ref, factor_ref, bound_ref, product, add)
    start = 0
    for ref in outs:
        blocks = ref.shape[0] // CLASSES
        ref[...] = total[pl.ds(start, blocks)].reshape(ref.shape).astype(ref.dtype)
        start += blocks


def gradient(first, step, meta, held, mine, other):
    send, keep = ((HALF, TILE), BF16), ((HALF, TILE), F32)
    return call(
        functools.partial(gradient_kernel, first, step),
        "far_gradient" if first else "near_gradient",
        [send, send] if first else [((LINE, TILE), F32), keep, send, send, keep],
        [smem()] * 3 + [vmem()] * 3,
        [
            VMEM((256 - FAR if first else FAR, CLASSES, TILE), F32),
            VMEM((ROW_BLOCKS, CLASSES, TILE), BF16),
        ],
        LIMIT,
        None if first else COST,
    )(*meta, held, mine, other)


def relay_kernel(keep_ref, came_ref, out_ref):
    out_ref[...] = (keep_ref[...] + came_ref[...].astype(F32)).astype(BF16)


def relay(keep, came):
    return call(relay_kernel, "relay", [((HALF, TILE), BF16)], [vmem()] * 2)(keep, came)[0]


def fold_kernel(own_ref, low_a, low_b, high_a, high_b, near_ref, *far_refs):
    for i in range(4):
        a_ref, b_ref = ((low_a, low_b), (high_a, high_b))[i // 2]
        rows = pl.ds(i % 2 * PIECE, PIECE)
        value = own_ref[pl.ds(i * PIECE, PIECE), :] + (
            a_ref[rows, :].astype(F32) + b_ref[rows, :].astype(F32)
        )
        if i == 0:
            near_ref[...] = value
        else:
            far_refs[i - 1][...] = value.astype(BF16)


def fold(own, *received):
    far = ((PIECE, TILE), BF16)
    return call(
        fold_kernel, "fold", [((PIECE, TILE), F32), far, far, far], [vmem()] * 5
    )(own, *received)


def update_kernel(step, rate_ref, w_ref, near_ref, a_ref, b_ref, c_ref, out_ref, *wide_ref):
    rate = rate_ref[step]
    for b in range(OWN_BLOCKS):
        rows = pl.ds(b * CLASSES, CLASSES)
        value = near_ref[rows, :] + (
            a_ref[rows, :].astype(F32) + b_ref[rows, :].astype(F32) + c_ref[rows, :].astype(F32)
        )
        new = w_ref[:, pl.ds(b * TILE, TILE)] - rate * value
        out_ref[:, pl.ds(b * TILE, TILE)] = new
        for ref in wide_ref:
            ref[rows, :] = new.astype(BF16)


def update(step, rate, weights, near, received, last):
    outs = [(weights.shape, F32)]
    if not last:
        outs.append(((PIECE, TILE), BF16))
    return call(
        functools.partial(update_kernel, step), "update", outs, [smem()] + [vmem()] * 5
    )(rate, weights, near, *received)


def per_device(
    tiles, tile_scales, tile_rows, tile_cols, tile_counts, labels, learning_rate, weights
):
    steps = tiles.shape[0]
    place = lax.axis_index("rows")
    core = lax.axis_index("cols") % 2
    z, y = place // 4, place % 4
    columns = tile_cols.reshape(steps, SLOTS)
    owner, within = columns // OWN_BLOCKS, columns % OWN_BLOCKS
    dz, dy = z - owner // 4, y - owner % 4
    i, j = dz & 3, dy & 3
    piece = j * 4 + i
    i, j = -dz & 3, -dy & 3
    line = jnp.where(j == 2, 3, jnp.where(j == 3, 2, j))
    places = jnp.stack([piece, line * 4 + i]) * OWN_BLOCKS + within
    block = (tile_rows.reshape(steps, SLOTS) + OWN_ROW_BLOCKS * core) & (ROW_BLOCKS - 1)
    slots = jnp.arange(SLOTS, dtype=jnp.int32)
    dead = slots >= tile_counts.reshape(steps, 1)
    run = jnp.where(dead, 2, jnp.stack([j < 0, j != 2]).astype(jnp.int32)).reshape(-1, SLOTS)
    code = (places + (block << 8) + (slots << 11)).reshape(-1, SLOTS)
    scales = jnp.broadcast_to(tile_scales.reshape(1, steps, SLOTS), (2, steps, SLOTS))
    mine, others = run[:, :, None], run[:, None, :]
    ahead = (others < mine) | ((others == mine) & (slots[None, :] < slots[:, None]))
    rank = jnp.sum(ahead.astype(jnp.int32), axis=2)
    moved = rank[:, None, :] == slots[None, :, None]
    code = jnp.sum(jnp.where(moved, code[:, None, :], 0), axis=2).reshape(-1)
    factor = jnp.sum(jnp.where(moved, scales.reshape(-1, 1, SLOTS), 0.0), axis=2).reshape(-1)
    bound = jnp.sum((run[:, None, :] <= jnp.arange(2)[None, :, None]).astype(jnp.int32), axis=2)
    meta = (code, factor, bound.reshape(-1))
    owned = labels.shape[1] // lax.axis_size("cols")
    start = lax.axis_index("cols") * owned

    losses = []
    wide = to_blocks(weights)
    for step in range(steps):
        pieces = {(0, 0): wide}
        for j in (3, 1, 2):
            pieces[j, 0] = y_shift(wide, j)
        for i in (3, 1, 2):
            pieces[0, i] = z_shift(wide, i)
        for i in (3, 1, 2):
            for j in (3, 1, 2):
                pieces[j, i] = y_shift(pieces[0, i], j)
        pieces = [pieces[j, i] for j in range(4) for i in range(4)]
        mine, other, held = partial_logits(step, meta, tiles, pieces)
        mine = mine + flip(other, 1)
        mine = mine + flip(mine, 2)
        parts = [mine] + [x_shift(mine, k) for k in (1, 2, 3)]
        mine, loss = classify(step, core.reshape(1), parts, labels)
        losses.append(loss)
        other = flip(mine, 1)
        far_low, far_high = gradient(True, step, meta, held, mine, other)
        via_low, via_high = y_shift(far_low, 1), y_shift(far_high, -1)
        own, up_keep, up_send, down_send, down_keep = gradient(
            False, step, meta, held, mine, other
        )
        high_a, low_a = y_shift(up_send, 1), y_shift(down_send, -1)
        low_b = y_shift(relay(up_keep, via_low), 1)
        high_b = y_shift(relay(down_keep, via_high), -1)
        near, *far = fold(own, low_a, low_b, high_a, high_b)
        received = [z_shift(far[k - 1], k) for k in (1, 2, 3)]
        weights, *wide = update(
            step, learning_rate, weights, near, received, step == steps - 1
        )
        wide = wide[0] if wide else None

    loss = jnp.stack(losses)
    there = flip(loss, 1)
    first = core == 0
    loss = jnp.concatenate([jnp.where(first, loss, there), jnp.where(first, there, loss)], axis=1)
    loss = lax.dynamic_slice_in_dim(loss.reshape(steps, -1), start, owned, axis=1)
    return weights, loss


def solution(mesh):
    return jax.shard_map(
        per_device,
        mesh=mesh,
        in_specs=(
            P(None, "rows", "cols", None, None, None),
            P(None, "rows", "cols", None),
            P(None, "rows", "cols", None),
            P(None, "rows", "cols", None),
            P(None, "rows", "cols"),
            P(None, "rows"),
            P(),
            P(None, ("cols", "rows")),
        ),
        out_specs=(P(None, ("cols", "rows")), P(None, ("rows", "cols"))),
        check_vma=False,
    )
```

```python
import functools

import jax
import jax.numpy as jnp
from jax import lax
from jax.experimental import pallas as pl
from jax.experimental.pallas import tpu as pltpu
from jax.sharding import PartitionSpec as P

CLASSES = 32
TILE = 128
SLOTS = 128
GROUP = 16
RUNS = 2
FIRST_PIECE = (0, 10, 16)
PIECE_REFS = (10, 6)
FAR = 192
ROW_BLOCKS = 8
OWN_ROW_BLOCKS = 4
OWN_BLOCKS = 16
PIECE = OWN_BLOCKS * CLASSES
LINE = 4 * PIECE
HALF = 3 * PIECE // 2
LIMIT = 20 * 1024 * 1024
SLOT_LIMIT = 46 * 1024 * 1024

STEPS = 2
VMEM = pltpu.VMEM
COST = pl.CostEstimate(flops=1 << 30, bytes_accessed=1 << 23, transcendentals=0)
F32 = jnp.float32
BF16 = jnp.bfloat16


def y_shift(value, k):
    perm = [(z * 4 + y, z * 4 + (y + k) % 4) for z in range(4) for y in range(4)]
    return lax.ppermute(value, "rows", perm)


def z_shift(value, k):
    perm = [(z * 4 + y, (z + k) % 4 * 4 + y) for z in range(4) for y in range(4)]
    return lax.ppermute(value, "rows", perm)


def x_shift(value, k):
    perm = [(x * 4 + j, (x + k) % 4 * 4 + j) for x in range(4) for j in range(4)]
    return lax.ppermute(value, "cols", perm)


def flip(value, bit):
    return lax.ppermute(value, "cols", [(i, i ^ bit) for i in range(16)])


def vmem():
    return pl.BlockSpec(memory_space=VMEM)


def smem():
    return pl.BlockSpec(memory_space=pltpu.SMEM)


def hbm():
    return pl.BlockSpec(memory_space=pltpu.HBM)


def call(kernel, name, outs, ins, scratch=(), limit=LIMIT, cost=None):
    return pl.pallas_call(
        kernel,
        out_shape=[jax.ShapeDtypeStruct(shape, dtype) for shape, dtype in outs],
        in_specs=ins,
        out_specs=[vmem()] * len(outs),
        scratch_shapes=list(scratch),
        compiler_params=pltpu.CompilerParams(vmem_limit_bytes=limit),
        cost_estimate=cost,
        name=name,
    )


def block_kernel(w_ref, out_ref):
    for b in range(OWN_BLOCKS):
        out_ref[pl.ds(b * CLASSES, CLASSES), :] = w_ref[:, pl.ds(b * TILE, TILE)].astype(BF16)


def to_blocks(weights):
    return call(block_kernel, "to_blocks", [((PIECE, TILE), BF16)], [vmem()])(weights)[0]


def over_slots(order, step, run, code_ref, factor_ref, bound_ref, product, add):
    row = order * STEPS + step
    low = 0 if run == 0 else bound_ref[RUNS * row + run - 1]
    high = bound_ref[RUNS * row + run]

    def body(group, carry):
        codes, factors = [], []
        for u in range(GROUP):
            place = low + group * GROUP + u
            entry = row * SLOTS + jnp.minimum(place, SLOTS - 1)
            codes.append(code_ref[entry])
            factors.append(jnp.where(place < high, factor_ref[entry], 0.0))
        products = [product(code & 255, (code >> 8) & 7, code >> 11) for code in codes]
        for code, factor, value in zip(codes, factors, products):
            add(code & 255, (code >> 8) & 7, factor * value)
        return carry

    lax.fori_loop(0, (high - low + GROUP - 1) // GROUP, body, 0)


def logits_kernel(run, step, code_ref, factor_ref, bound_ref, tiles_ref, *rest):
    first, count = FIRST_PIECE[run], FIRST_PIECE[run + 1] - FIRST_PIECE[run]
    pieces, rest = rest[: PIECE_REFS[run]], rest[PIECE_REFS[run] :]
    if run == 0:
        total, held, wide, sem = rest
        copy = pltpu.make_async_copy(tiles_ref.at[step, 0, 0], held, sem)
        copy.start()
        total[...] = jnp.zeros_like(total)
    else:
        held, before, total, wide = tiles_ref, rest[0], rest[3], rest[4]
        total[...] = before[...]
    start = 0
    for piece in pieces:
        blocks = piece.shape[0] // CLASSES
        wide[pl.ds(start, blocks)] = piece[...].reshape(blocks, CLASSES, TILE)
        start += blocks
    if run == 0:
        copy.wait()

    def product(place, block, slot):
        place = jnp.clip(place - first * OWN_BLOCKS, 0, count * OWN_BLOCKS - 1)
        return lax.dot_general(
            wide[place], held[slot], (((1,), (1,)), ((), ())), preferred_element_type=F32
        )

    def add(place, block, value):
        total[block] += value

    over_slots(0, step, run, code_ref, factor_ref, bound_ref, product, add)
    if run == 1:
        rest[1][...] = total[pl.ds(0, OWN_ROW_BLOCKS)]
        rest[2][...] = total[pl.ds(OWN_ROW_BLOCKS, OWN_ROW_BLOCKS)]


def partial_logits(run, step, meta, tiles, pieces, *before):
    half, whole = ((OWN_ROW_BLOCKS, CLASSES, TILE), F32), ((ROW_BLOCKS, CLASSES, TILE), F32)
    blocks = (FIRST_PIECE[run + 1] - FIRST_PIECE[run]) * OWN_BLOCKS
    wide = VMEM((blocks, CLASSES, TILE), BF16)
    return call(
        functools.partial(logits_kernel, run, step),
        "logits_run%d" % run,
        ([whole, ((SLOTS, TILE, TILE), BF16)], [half, half])[run],
        [smem()] * 3 + [vmem() if run else hbm()] + [vmem()] * (len(pieces) + len(before)),
        ([wide, pltpu.SemaphoreType.DMA], [VMEM(whole[0], F32), wide])[run],
        LIMIT if run else SLOT_LIMIT,
    )(*meta, tiles, *pieces, *before)


def classify_kernel(step, core_ref, a_ref, b_ref, c_ref, d_ref, label_ref, *outs):
    residual_ref, loss_ref = outs
    for block in range(OWN_ROW_BLOCKS):
        scores = (a_ref[block] + b_ref[block]) + (c_ref[block] + d_ref[block])
        first = (core_ref[0] * OWN_ROW_BLOCKS + block) * TILE
        label = label_ref[pl.ds(step, 1), pl.ds(pl.multiple_of(first, TILE), TILE)]
        hit = lax.broadcasted_iota(jnp.int32, (CLASSES, TILE), 0) == label
        exps = jnp.exp(scores)
        denominator = jnp.sum(exps, axis=0, keepdims=True)
        picked = jnp.sum(jnp.where(hit, scores, 0.0), axis=0, keepdims=True)
        loss_ref[pl.ds(block, 1), :] = jnp.log(denominator) - picked
        residual_ref[block] = (exps / denominator - hit.astype(F32)).astype(BF16)


def classify(step, core, parts, labels):
    return call(
        functools.partial(classify_kernel, step),
        "classify",
        [((OWN_ROW_BLOCKS, CLASSES, TILE), BF16), ((OWN_ROW_BLOCKS, TILE), F32)],
        [smem()] + [vmem()] * 5,
    )(core, *parts, labels)


def gradient_kernel(first, step, code_ref, factor_ref, bound_ref, held, mine_ref, other_ref, *rest):
    outs, (total, residual) = rest[:-2], rest[-2:]
    residual[pl.ds(0, OWN_ROW_BLOCKS)] = mine_ref[...]
    residual[pl.ds(OWN_ROW_BLOCKS, OWN_ROW_BLOCKS)] = other_ref[...]
    total[...] = jnp.zeros_like(total)

    def product(place, block, slot):
        return lax.dot_general(
            residual[block], held[slot], (((1,), (0,)), ((), ())), preferred_element_type=F32
        )

    def add(place, block, value):
        place = jnp.maximum(place - FAR, 0) if first else jnp.minimum(place, FAR - 1)
        total[place] += value

    over_slots(1, step, 0 if first else 1, code_ref, factor_ref, bound_ref, product, add)
    start = 0
    for ref in outs:
        blocks = ref.shape[0] // CLASSES
        ref[...] = total[pl.ds(start, blocks)].reshape(ref.shape).astype(ref.dtype)
        start += blocks


def gradient(first, step, meta, held, mine, other):
    send, keep, same = ((HALF, TILE), BF16), ((HALF, TILE), F32), ((PIECE, TILE), BF16)
    return call(
        functools.partial(gradient_kernel, first, step),
        "far_gradient" if first else "near_gradient",
        [same, send, send] if first else [((LINE, TILE), F32), same, keep, send, same, send, keep],
        [smem()] * 3 + [vmem()] * 3,
        [
            VMEM((256 - FAR if first else FAR, CLASSES, TILE), F32),
            VMEM((ROW_BLOCKS, CLASSES, TILE), BF16),
        ],
        LIMIT,
        None if first else COST,
    )(*meta, held, mine, other)


def relay_kernel(keep_ref, came_ref, out_ref):
    out_ref[...] = (keep_ref[...] + came_ref[...].astype(F32)).astype(BF16)


def relay(keep, came):
    return call(relay_kernel, "relay", [((HALF, TILE), BF16)], [vmem()] * 2)(keep, came)[0]


def fold_kernel(own_ref, low_a, low_b, high_a, high_b, *rest):
    for came, out in zip(rest[:3], rest[6:]):
        out[...] = came[...]
    quarter = HALF // 3
    for part in range(6):
        a_ref, b_ref = ((low_a, low_b), (high_a, high_b))[part // 3]
        rows = pl.ds(part % 3 * quarter, quarter)
        value = own_ref[pl.ds(PIECE + part * quarter, quarter), :] + (
            a_ref[rows, :].astype(F32) + b_ref[rows, :].astype(F32)
        )
        rest[3 + part // 2][pl.ds(part % 2 * quarter, quarter), :] = value.astype(BF16)


def fold(own, *received):
    piece = ((PIECE, TILE), BF16)
    return call(fold_kernel, "fold", [piece] * 6, [vmem()] * 8)(own, *received)


def update_kernel(step, rate_ref, w_ref, near_ref, *rest):
    received, out_ref, wide_ref = rest[:6], rest[6], rest[7:]
    rate = rate_ref[step]
    for b in range(OWN_BLOCKS):
        rows = pl.ds(b * CLASSES, CLASSES)
        value = near_ref[rows, :]
        for ref in received:
            value += ref[rows, :].astype(F32)
        new = w_ref[:, pl.ds(b * TILE, TILE)] - rate * value
        out_ref[:, pl.ds(b * TILE, TILE)] = new
        for ref in wide_ref:
            ref[rows, :] = new.astype(BF16)


def update(step, rate, weights, near, received, last):
    outs = [(weights.shape, F32)]
    if not last:
        outs.append(((PIECE, TILE), BF16))
    return call(
        functools.partial(update_kernel, step), "update", outs, [smem()] + [vmem()] * 8
    )(rate, weights, near, *received)


def per_device(
    tiles, tile_scales, tile_rows, tile_cols, tile_counts, labels, learning_rate, weights
):
    steps = tiles.shape[0]
    place = lax.axis_index("rows")
    core = lax.axis_index("cols") % 2
    z, y = place // 4, place % 4
    columns = tile_cols.reshape(steps, SLOTS)
    owner, within = columns // OWN_BLOCKS, columns % OWN_BLOCKS
    dz, dy = z - owner // 4, y - owner % 4
    i, j = dz & 3, dy & 3
    late = (j != 0) & ((i == 1) | (i == 2))
    piece = jnp.where(late, 9 + (j - 1) * 2 + i, jnp.where(j == 0, i, 2 + j * 2 + (i == 3)))
    run = late.astype(jnp.int32)
    i, j = -dz & 3, -dy & 3
    line = jnp.where(j == 2, 3, jnp.where(j == 3, 2, j))
    places = jnp.stack([piece, line * 4 + i]) * OWN_BLOCKS + within
    block = (tile_rows.reshape(steps, SLOTS) + OWN_ROW_BLOCKS * core) & (ROW_BLOCKS - 1)
    slots = jnp.arange(SLOTS, dtype=jnp.int32)
    dead = slots >= tile_counts.reshape(steps, 1)
    run = jnp.where(dead, RUNS, jnp.stack([run, (j != 2).astype(jnp.int32)])).reshape(-1, SLOTS)
    code = (places + (block << 8) + (slots << 11)).reshape(-1, SLOTS)
    scales = jnp.broadcast_to(tile_scales.reshape(1, steps, SLOTS), (2, steps, SLOTS))
    mine, others = run[:, :, None], run[:, None, :]
    ahead = (others < mine) | ((others == mine) & (slots[None, :] < slots[:, None]))
    rank = jnp.sum(ahead.astype(jnp.int32), axis=2)
    moved = rank[:, None, :] == slots[None, :, None]
    code = jnp.sum(jnp.where(moved, code[:, None, :], 0), axis=2).reshape(-1)
    factor = jnp.sum(jnp.where(moved, scales.reshape(-1, 1, SLOTS), 0.0), axis=2).reshape(-1)
    bound = jnp.sum((run[:, None, :] <= jnp.arange(RUNS)[None, :, None]).astype(jnp.int32), axis=2)
    meta = (code, factor, bound.reshape(-1))
    owned = labels.shape[1] // lax.axis_size("cols")
    start = lax.axis_index("cols") * owned

    losses = []
    wide = to_blocks(weights)
    for step in range(steps):
        pieces = {(0, 0): wide}
        for j in (2, 1, 3):
            pieces[j, 0] = y_shift(wide, j)
        for i in (2, 1, 3):
            pieces[0, i] = z_shift(wide, i)
        for i in (2, 1, 3):
            for j in (2, 1, 3):
                pieces[j, i] = y_shift(pieces[0, i], j)
        early = [(0, 0), (0, 1), (0, 2), (0, 3), (1, 0), (1, 3), (2, 0), (2, 3), (3, 0), (3, 3)]
        late = [(1, 1), (1, 2), (2, 1), (2, 2), (3, 1), (3, 2)]
        total, held = partial_logits(0, step, meta, tiles, [pieces[k] for k in early])
        mine, other = partial_logits(1, step, meta, held, [pieces[k] for k in late], total)
        mine = mine + flip(other, 1)
        mine = mine + flip(mine, 2)
        parts = [mine] + [x_shift(mine, k) for k in (1, 2, 3)]
        mine, loss = classify(step, core.reshape(1), parts, labels)
        losses.append(loss)
        other = flip(mine, 1)
        far_same, far_low, far_high = gradient(True, step, meta, held, mine, other)
        via_low, via_high = y_shift(far_low, 1), y_shift(far_high, -1)
        own, up_same, up_keep, up_send, down_same, down_send, down_keep = gradient(
            False, step, meta, held, mine, other
        )
        high_a, low_a = y_shift(up_send, 1), y_shift(down_send, -1)
        low_b = y_shift(relay(up_keep, via_low), 1)
        high_b = y_shift(relay(down_keep, via_high), -1)
        sums = fold(own, low_a, low_b, high_a, high_b, far_same, up_same, down_same)
        received = [z_shift(sums[i - 1], i) for i in (1, 2, 3)]
        received += [y_shift(value, j) for value, j in zip(sums[3:], (2, 1, -1))]
        weights, *wide = update(
            step, learning_rate, weights, own, received, step == steps - 1
        )
        wide = wide[0] if wide else None

    loss = jnp.stack(losses)
    there = flip(loss, 1)
    first = core == 0
    loss = jnp.concatenate([jnp.where(first, loss, there), jnp.where(first, there, loss)], axis=1)
    loss = lax.dynamic_slice_in_dim(loss.reshape(steps, -1), start, owned, axis=1)
    return weights, loss


def solution(mesh):
    return jax.shard_map(
        per_device,
        mesh=mesh,
        in_specs=(
            P(None, "rows", "cols", None, None, None),
            P(None, "rows", "cols", None),
            P(None, "rows", "cols", None),
            P(None, "rows", "cols", None),
            P(None, "rows", "cols"),
            P(None, "rows"),
            P(),
            P(None, ("cols", "rows")),
        ),
        out_specs=(P(None, ("cols", "rows")), P(None, ("rows", "cols"))),
        check_vma=False,
    )
```

```python
import functools

import jax
import jax.numpy as jnp
from jax import lax
from jax.experimental import pallas as pl
from jax.experimental.pallas import tpu as pltpu
from jax.sharding import PartitionSpec as P

CLASSES = 32
TILE = 128
SLOTS = 128
GROUP = 16
RUNS = 2
FIRST_PIECE = (0, 10, 16)
PIECE_REFS = (10, 6)
FAR = 192
ROW_BLOCKS = 8
OWN_ROW_BLOCKS = 4
OWN_BLOCKS = 16
PIECE = OWN_BLOCKS * CLASSES
LINE = 4 * PIECE
HALF = 3 * PIECE // 2
LIMIT = 20 * 1024 * 1024
SLOT_LIMIT = 46 * 1024 * 1024

STEPS = 2
VMEM = pltpu.VMEM
COST = pl.CostEstimate(flops=1 << 30, bytes_accessed=1 << 23, transcendentals=0)
F32 = jnp.float32
BF16 = jnp.bfloat16


def y_shift(value, k):
    perm = [(z * 4 + y, z * 4 + (y + k) % 4) for z in range(4) for y in range(4)]
    return lax.ppermute(value, "rows", perm)


def z_shift(value, k):
    perm = [(z * 4 + y, (z + k) % 4 * 4 + y) for z in range(4) for y in range(4)]
    return lax.ppermute(value, "rows", perm)


def x_shift(value, k):
    perm = [(x * 4 + j, (x + k) % 4 * 4 + j) for x in range(4) for j in range(4)]
    return lax.ppermute(value, "cols", perm)


def flip(value, bit):
    return lax.ppermute(value, "cols", [(i, i ^ bit) for i in range(16)])


def vmem():
    return pl.BlockSpec(memory_space=VMEM)


def smem():
    return pl.BlockSpec(memory_space=pltpu.SMEM)


def hbm():
    return pl.BlockSpec(memory_space=pltpu.HBM)


def call(kernel, name, outs, ins, scratch=(), limit=LIMIT, cost=None):
    return pl.pallas_call(
        kernel,
        out_shape=[jax.ShapeDtypeStruct(shape, dtype) for shape, dtype in outs],
        in_specs=ins,
        out_specs=[vmem()] * len(outs),
        scratch_shapes=list(scratch),
        compiler_params=pltpu.CompilerParams(vmem_limit_bytes=limit),
        cost_estimate=cost,
        name=name,
    )


def block_kernel(w_ref, out_ref):
    for b in range(OWN_BLOCKS):
        out_ref[pl.ds(b * CLASSES, CLASSES), :] = w_ref[:, pl.ds(b * TILE, TILE)].astype(BF16)


def to_blocks(weights):
    return call(block_kernel, "to_blocks", [((PIECE, TILE), BF16)], [vmem()])(weights)[0]


def over_slots(order, step, run, code_ref, factor_ref, bound_ref, product, add, size=GROUP):
    row = order * STEPS + step
    low = 0 if run == 0 else bound_ref[RUNS * row + run - 1]
    high = bound_ref[RUNS * row + run]

    def body(group, carry):
        codes, factors = [], []
        for u in range(size):
            place = low + group * size + u
            entry = row * SLOTS + jnp.minimum(place, SLOTS - 1)
            codes.append(code_ref[entry])
            factors.append(jnp.where(place < high, factor_ref[entry], 0.0))
        products = [product(code & 255, (code >> 8) & 7, code >> 11) for code in codes]
        for code, factor, value in zip(codes, factors, products):
            add(code & 255, (code >> 8) & 7, factor * value)
        return carry

    lax.fori_loop(0, (high - low + size - 1) // size, body, 0)


def logits_kernel(run, step, code_ref, factor_ref, bound_ref, tiles_ref, *rest):
    first, count = FIRST_PIECE[run], FIRST_PIECE[run + 1] - FIRST_PIECE[run]
    pieces, rest = rest[: PIECE_REFS[run]], rest[PIECE_REFS[run] :]
    if run == 0:
        total, held, wide, sem = rest
        copy = pltpu.make_async_copy(tiles_ref.at[step, 0, 0], held, sem)
        copy.start()
        total[...] = jnp.zeros_like(total)
    else:
        held, before, total, wide = tiles_ref, rest[0], rest[3], rest[4]
        total[...] = before[...]
    start = 0
    for piece in pieces:
        blocks = piece.shape[0] // CLASSES
        wide[pl.ds(start, blocks)] = piece[...].reshape(blocks, CLASSES, TILE)
        start += blocks
    if run == 0:
        copy.wait()

    def product(place, block, slot):
        place = jnp.clip(place - first * OWN_BLOCKS, 0, count * OWN_BLOCKS - 1)
        return lax.dot_general(
            wide[place], held[slot], (((1,), (1,)), ((), ())), preferred_element_type=F32
        )

    def add(place, block, value):
        total[block] += value

    over_slots(0, step, run, code_ref, factor_ref, bound_ref, product, add)
    if run == 1:
        rest[1][...] = total[pl.ds(0, OWN_ROW_BLOCKS)]
        rest[2][...] = total[pl.ds(OWN_ROW_BLOCKS, OWN_ROW_BLOCKS)]


def partial_logits(run, step, meta, tiles, pieces, *before):
    half, whole = ((OWN_ROW_BLOCKS, CLASSES, TILE), F32), ((ROW_BLOCKS, CLASSES, TILE), F32)
    blocks = (FIRST_PIECE[run + 1] - FIRST_PIECE[run]) * OWN_BLOCKS
    wide = VMEM((blocks, CLASSES, TILE), BF16)
    return call(
        functools.partial(logits_kernel, run, step),
        "logits_run%d" % run,
        ([whole, ((SLOTS, TILE, TILE), BF16)], [half, half])[run],
        [smem()] * 3 + [vmem() if run else hbm()] + [vmem()] * (len(pieces) + len(before)),
        ([wide, pltpu.SemaphoreType.DMA], [VMEM(whole[0], F32), wide])[run],
        LIMIT if run else SLOT_LIMIT,
    )(*meta, tiles, *pieces, *before)


def classify_kernel(step, core_ref, a_ref, b_ref, c_ref, d_ref, label_ref, *outs):
    residual_ref, loss_ref = outs
    for block in range(OWN_ROW_BLOCKS):
        scores = (a_ref[block] + b_ref[block]) + (c_ref[block] + d_ref[block])
        first = (core_ref[0] * OWN_ROW_BLOCKS + block) * TILE
        label = label_ref[pl.ds(step, 1), pl.ds(pl.multiple_of(first, TILE), TILE)]
        hit = lax.broadcasted_iota(jnp.int32, (CLASSES, TILE), 0) == label
        exps = jnp.exp(scores)
        denominator = jnp.sum(exps, axis=0, keepdims=True)
        picked = jnp.sum(jnp.where(hit, scores, 0.0), axis=0, keepdims=True)
        loss_ref[pl.ds(block, 1), :] = jnp.log(denominator) - picked
        residual_ref[block] = (exps / denominator - hit.astype(F32)).astype(BF16)


def classify(step, core, parts, labels):
    return call(
        functools.partial(classify_kernel, step),
        "classify",
        [((OWN_ROW_BLOCKS, CLASSES, TILE), BF16), ((OWN_ROW_BLOCKS, TILE), F32)],
        [smem()] + [vmem()] * 5,
    )(core, *parts, labels)


def gradient_kernel(first, step, code_ref, factor_ref, bound_ref, held, mine_ref, other_ref, *rest):
    outs, (total, residual) = rest[:-2], rest[-2:]
    residual[pl.ds(0, OWN_ROW_BLOCKS)] = mine_ref[...]
    residual[pl.ds(OWN_ROW_BLOCKS, OWN_ROW_BLOCKS)] = other_ref[...]
    total[...] = jnp.zeros_like(total)

    def product(place, block, slot):
        return lax.dot_general(
            residual[block], held[slot], (((1,), (0,)), ((), ())), preferred_element_type=F32
        )

    def add(place, block, value):
        place = jnp.maximum(place - FAR, 0) if first else jnp.minimum(place, FAR - 1)
        total[place] += value

    over_slots(
        1, step, 0 if first else 1, code_ref, factor_ref, bound_ref, product, add, 2 * GROUP
    )
    start = 0
    for ref in outs:
        blocks = ref.shape[0] // CLASSES
        ref[...] = total[pl.ds(start, blocks)].reshape(ref.shape).astype(ref.dtype)
        start += blocks


def gradient(first, step, meta, held, mine, other):
    send, keep, same = ((HALF, TILE), BF16), ((HALF, TILE), F32), ((PIECE, TILE), BF16)
    return call(
        functools.partial(gradient_kernel, first, step),
        "far_gradient" if first else "near_gradient",
        [same, send, send] if first else [((LINE, TILE), F32), same, keep, send, same, send, keep],
        [smem()] * 3 + [vmem()] * 3,
        [
            VMEM((256 - FAR if first else FAR, CLASSES, TILE), F32),
            VMEM((ROW_BLOCKS, CLASSES, TILE), BF16),
        ],
        LIMIT,
        None if first else COST,
    )(*meta, held, mine, other)


def relay_kernel(keep_ref, came_ref, out_ref):
    out_ref[...] = (keep_ref[...] + came_ref[...].astype(F32)).astype(BF16)


def relay(keep, came):
    return call(relay_kernel, "relay", [((HALF, TILE), BF16)], [vmem()] * 2)(keep, came)[0]


def fold_kernel(own_ref, low_a, low_b, high_a, high_b, *rest):
    for came, out in zip(rest[:3], rest[6:]):
        out[...] = came[...]
    quarter = HALF // 3
    for part in range(6):
        a_ref, b_ref = ((low_a, low_b), (high_a, high_b))[part // 3]
        rows = pl.ds(part % 3 * quarter, quarter)
        value = own_ref[pl.ds(PIECE + part * quarter, quarter), :] + (
            a_ref[rows, :].astype(F32) + b_ref[rows, :].astype(F32)
        )
        rest[3 + part // 2][pl.ds(part % 2 * quarter, quarter), :] = value.astype(BF16)


def fold(own, *received):
    piece = ((PIECE, TILE), BF16)
    return call(fold_kernel, "fold", [piece] * 6, [vmem()] * 8)(own, *received)


def update_kernel(step, rate_ref, w_ref, near_ref, *rest):
    received, out_ref, wide_ref = rest[:6], rest[6], rest[7:]
    rate = rate_ref[step]
    for b in range(OWN_BLOCKS):
        rows = pl.ds(b * CLASSES, CLASSES)
        value = near_ref[rows, :]
        for ref in received:
            value += ref[rows, :].astype(F32)
        new = w_ref[:, pl.ds(b * TILE, TILE)] - rate * value
        out_ref[:, pl.ds(b * TILE, TILE)] = new
        for ref in wide_ref:
            ref[rows, :] = new.astype(BF16)


def update(step, rate, weights, near, received, last):
    outs = [(weights.shape, F32)]
    if not last:
        outs.append(((PIECE, TILE), BF16))
    return call(
        functools.partial(update_kernel, step), "update", outs, [smem()] + [vmem()] * 8
    )(rate, weights, near, *received)


def per_device(
    tiles, tile_scales, tile_rows, tile_cols, tile_counts, labels, learning_rate, weights
):
    steps = tiles.shape[0]
    place = lax.axis_index("rows")
    core = lax.axis_index("cols") % 2
    z, y = place // 4, place % 4
    columns = tile_cols.reshape(steps, SLOTS)
    owner, within = columns // OWN_BLOCKS, columns % OWN_BLOCKS
    dz, dy = z - owner // 4, y - owner % 4
    i, j = dz & 3, dy & 3
    late = (j != 0) & ((i == 1) | (i == 2))
    piece = jnp.where(late, 9 + (j - 1) * 2 + i, jnp.where(j == 0, i, 2 + j * 2 + (i == 3)))
    run = late.astype(jnp.int32)
    i, j = -dz & 3, -dy & 3
    line = jnp.where(j == 2, 3, jnp.where(j == 3, 2, j))
    places = jnp.stack([piece, line * 4 + i]) * OWN_BLOCKS + within
    block = (tile_rows.reshape(steps, SLOTS) + OWN_ROW_BLOCKS * core) & (ROW_BLOCKS - 1)
    slots = jnp.arange(SLOTS, dtype=jnp.int32)
    dead = slots >= tile_counts.reshape(steps, 1)
    run = jnp.where(dead, RUNS, jnp.stack([run, (j != 2).astype(jnp.int32)])).reshape(-1, SLOTS)
    code = (places + (block << 8) + (slots << 11)).reshape(-1, SLOTS)
    scales = jnp.broadcast_to(tile_scales.reshape(1, steps, SLOTS), (2, steps, SLOTS))
    mine, others = run[:, :, None], run[:, None, :]
    ahead = (others < mine) | ((others == mine) & (slots[None, :] < slots[:, None]))
    rank = jnp.sum(ahead.astype(jnp.int32), axis=2)
    moved = rank[:, None, :] == slots[None, :, None]
    code = jnp.sum(jnp.where(moved, code[:, None, :], 0), axis=2).reshape(-1)
    factor = jnp.sum(jnp.where(moved, scales.reshape(-1, 1, SLOTS), 0.0), axis=2).reshape(-1)
    bound = jnp.sum((run[:, None, :] <= jnp.arange(RUNS)[None, :, None]).astype(jnp.int32), axis=2)
    meta = (code, factor, bound.reshape(-1))
    owned = labels.shape[1] // lax.axis_size("cols")
    start = lax.axis_index("cols") * owned

    losses = []
    wide = to_blocks(weights)
    for step in range(steps):
        pieces = {(0, 0): wide}
        for j in (2, 1, 3):
            pieces[j, 0] = y_shift(wide, j)
        for i in (2, 1, 3):
            pieces[0, i] = z_shift(wide, i)
        for i in (2, 1, 3):
            for j in (2, 1, 3):
                pieces[j, i] = y_shift(pieces[0, i], j)
        early = [(0, 0), (0, 1), (0, 2), (0, 3), (1, 0), (1, 3), (2, 0), (2, 3), (3, 0), (3, 3)]
        late = [(1, 1), (1, 2), (2, 1), (2, 2), (3, 1), (3, 2)]
        total, held = partial_logits(0, step, meta, tiles, [pieces[k] for k in early])
        mine, other = partial_logits(1, step, meta, held, [pieces[k] for k in late], total)
        mine = mine + flip(other, 1)
        mine = mine + flip(mine, 2)
        parts = [mine] + [x_shift(mine, k) for k in (1, 2, 3)]
        mine, loss = classify(step, core.reshape(1), parts, labels)
        losses.append(loss)
        other = flip(mine, 1)
        far_same, far_low, far_high = gradient(True, step, meta, held, mine, other)
        via_low, via_high = y_shift(far_low, 1), y_shift(far_high, -1)
        own, up_same, up_keep, up_send, down_same, down_send, down_keep = gradient(
            False, step, meta, held, mine, other
        )
        high_a, low_a = y_shift(up_send, 1), y_shift(down_send, -1)
        low_b = y_shift(relay(up_keep, via_low), 1)
        high_b = y_shift(relay(down_keep, via_high), -1)
        sums = fold(own, low_a, low_b, high_a, high_b, far_same, up_same, down_same)
        received = [z_shift(sums[i - 1], i) for i in (1, 2, 3)]
        received += [y_shift(value, j) for value, j in zip(sums[3:], (2, 1, -1))]
        weights, *wide = update(
            step, learning_rate, weights, own, received, step == steps - 1
        )
        wide = wide[0] if wide else None

    loss = jnp.stack(losses)
    there = flip(loss, 1)
    first = core == 0
    loss = jnp.concatenate([jnp.where(first, loss, there), jnp.where(first, there, loss)], axis=1)
    loss = lax.dynamic_slice_in_dim(loss.reshape(steps, -1), start, owned, axis=1)
    return weights, loss


def solution(mesh):
    return jax.shard_map(
        per_device,
        mesh=mesh,
        in_specs=(
            P(None, "rows", "cols", None, None, None),
            P(None, "rows", "cols", None),
            P(None, "rows", "cols", None),
            P(None, "rows", "cols", None),
            P(None, "rows", "cols"),
            P(None, "rows"),
            P(),
            P(None, ("cols", "rows")),
        ),
        out_specs=(P(None, ("cols", "rows")), P(None, ("rows", "cols"))),
        check_vma=False,
    )
```
